32 devices in a mesh: dp: 4 (over x, core), ctx: 4 (over z), exp: 2 (over y).
Axes of the slice: x: 2, y: 2, z: 4, core: 2. Of those that a mesh axis runs over, the one named last changes fastest.
Arguments:
- block_input: bfloat16 [8, 1024, 768], P(('dp', 'exp'), 'ctx'), may hold values from -6 to 6
- out_cotangent: bfloat16 [8, 1024, 768], P(('dp', 'exp'), 'ctx'), may hold values from -6 to 6
- expert_ids: int32 [2, 8, 4, 256, 1], P(None, ('dp', 'exp'), 'ctx'), may hold values from 0 to 3; in each aligned block of 256 rows (0 to 255, 256 to 511, ..., all dimensions but the last counted through in order) at most 128 rows name the same one
- rel_buckets: int32 [2047], replicated, may hold values from 0 to 31
- bias_table: bfloat16 [32, 12], replicated, may hold values from -6 to 6
- gain_attn: bfloat16 [2, 768], P(None, 'dp'), may hold values from 0.5 to 1.5
- w_query: bfloat16 [2, 768, 768], P(None, 'dp'), may hold values from -0.21875 to 0.21875
- w_key: bfloat16 [2, 768, 768], P(None, 'dp'), may hold values from -0.21875 to 0.21875
- w_value: bfloat16 [2, 768, 768], P(None, 'dp'), may hold values from -0.21875 to 0.21875
- w_output: bfloat16 [2, 768, 768], P(None, 'dp'), may hold values from -3.5 to 3.5
- gain_ffn: bfloat16 [2, 768], P(None, 'dp'), may hold values from 0.5 to 1.5
- w_router: bfloat16 [2, 768, 4], P(None, 'dp'), may hold values from -0.109375 to 0.109375
- w_inner: bfloat16 [2, 4, 768, 3072], P(None, 'exp', 'dp'), may hold values from -0.21875 to 0.21875
- w_outer: bfloat16 [2, 4, 3072, 768], P(None, 'exp', 'dp'), may hold values from -0.75 to 0.75
Outputs:
- block_output: bfloat16 [8, 1024, 768], P(('dp', 'exp'), 'ctx')
- input_grad: float32 [8, 1024, 768], P(('dp', 'exp'), 'ctx')
- gain_attn_grad: float32 [2, 768], P(None, 'dp')
- w_query_grad: float32 [2, 768, 768], P(None, 'dp')
- w_key_grad: float32 [2, 768, 768], P(None, 'dp')
- w_value_grad: float32 [2, 768, 768], P(None, 'dp')
- w_output_grad: float32 [2, 768, 768], P(None, 'dp')
- gain_ffn_grad: float32 [2, 768], P(None, 'dp')
- w_router_grad: float32 [2, 768, 4], P(None, 'dp')
- w_inner_grad: float32 [2, 4, 768, 3072], P(None, 'exp', 'dp')
- w_outer_grad: float32 [2, 4, 3072, 768], P(None, 'exp', 'dp')
- bias_table_grad: float32 [32, 12], P(None, 'dp')
The draws below stay inside these ranges and needn't reach their ends.
Inputs may be any that keep to these rules, and one draw needn't show every extreme that they name: `expert_ids`: row r of group (g, c) is token r % 256 of block c of sequence g + r // 256. In each layer no expert is named by more than 128 of the rows of one group (g, c), a bound that some group reaches. `rel_buckets`: entry 1023 + j - i is the bucket of key position j seen from query position i.
All inputs are finite; a program needn't handle non-finite values.
Results may differ from the reference program's by a relative error of at most 0.035.
Values may be sent and summed in bfloat16 or wider, within the bound.
A program may use at most 320 MiB of HBM per device.

```python
import math
from functools import partial
import jax
import jax.numpy as jnp
import numpy as np
from jax import lax

D = 768
H = 12
DH = 64
FF = 3072
NB = 32
LAYERS = 2
SEQS = 1
BLK = 256
HD = 768
EXPERTS = 4
SEQ_LEN = 1024
NSEQ = 8
CAP = 128
N_DP = 4
N_CTX = 4
N_EXP = 2


def set_ends(values, stream_key, smallest, largest):
    shape = values.shape
    spot = [jax.random.randint(jax.random.fold_in(stream_key, axis), (), 0, shape[axis]) for axis in range(len(shape))]
    values = values.at[tuple(spot)].set(smallest)
    longest = shape.index(max(shape))
    spot[longest] = (spot[longest] + 1) % shape[longest]
    return values.at[tuple(spot)].set(largest)


def block_levels(key, dims, pieces, smallest, top_value):
    level, own = 1.0, jax.random.fold_in(key, 6)
    for dim, blocks in pieces:
        heights = jnp.exp(jax.random.uniform(jax.random.fold_in(own, dim), (blocks,), jnp.float32, smallest / len(pieces), top_value / len(pieces)))
        level = level * jnp.repeat(heights, dims[dim] // blocks).reshape([-1 if axis == dim else 1 for axis in range(len(dims))])
    return level


def routed_block(own_key, own, number, rows, amount, top, limit, slope):
    order = jax.random.permutation(own_key, amount)
    heavy_load, ordinary = load_shares(amount, rows * top, limit, slope, True), load_shares(amount, rows * top, limit, slope, False)
    places = jnp.arange(amount)

    def named(lengths, turn):
        used = int((lengths > 0).sum())
        fixed = max(1, used // 4)
        moved = fixed + (places - fixed + turn * (used - fixed)) % max(1, amount - fixed)
        return jnp.zeros((amount,), jnp.int32).at[order[jnp.where(places < fixed, places, moved)]].set(jnp.asarray(lengths, jnp.int32))

    lengths = jnp.where(number % 4 == 0, named(heavy_load, number // 4), named(ordinary, number - number // 4 - 1))
    mixed = jax.random.permutation(jax.random.fold_in(own, 3), amount)
    source_of, taker = mixed[0:amount // 2 * 2:2], mixed[1:amount // 2 * 2:2]
    slack = jnp.minimum(lengths[source_of] - 1, limit - lengths[taker]) // 2
    slack = jnp.where((source_of == order[0]) | (taker == order[0]) | (lengths[taker] == 0), 0, jnp.maximum(slack, 0))
    moved = jax.random.randint(jax.random.fold_in(own, 4), (amount // 2,), 0, 1 << 20) % (slack + 1)
    lengths = lengths.at[source_of].add(-moved).at[taker].add(moved)
    items = jnp.searchsorted(jnp.cumsum(lengths), jnp.arange(rows * top), side="right").astype(jnp.int32)
    table = items.reshape(top, rows).T
    table = table[jax.random.permutation(jax.random.fold_in(own, 1), rows)]
    turn = jax.random.randint(jax.random.fold_in(own, 2), (rows, 1), 0, top)
    return jnp.take_along_axis(table, (jnp.arange(top)[None, :] + turn) % top, axis=1)


def load_shares(amount, total, most, lean, full):
    weights = [(1 << 20) // math.isqrt(grade ** lean) + 1 for grade in range(1, amount + 1)]
    largest = most if full else min(most, max(-(-total // amount), total * weights[0] // sum(weights)))
    least = 1 if total - largest >= amount - 1 else 0
    holding, spare = [largest] + [least] * (amount - 1), total - largest - least * (amount - 1)
    while spare > 0:
        movable = [i for i in range(1, amount) if holding[i] < largest] or [i for i in range(1, amount) if holding[i] < most]
        mass, left = sum([weights[i] for i in movable]), spare
        for i in movable:
            addition = min(most - holding[i], max(1, left * weights[i] // mass), spare)
            holding[i] = holding[i] + addition
            spare = spare - addition
    return np.array(holding)


def normal_values(own_key, shape, width, limit, cuts=(), kind=jnp.bfloat16):
    factor_of = block_levels(own_key, shape, cuts, -0.22, 0.18) if cuts else 1.0
    entries = jax.random.normal(own_key, shape, jnp.float32) * width * factor_of
    return jnp.minimum(jnp.maximum(entries, -limit), limit).astype(kind)


def setup_inputs(seed: int = 0) -> dict:
    key_list = jax.random.split(jax.random.key(seed), 15)
    block_input = normal_values(key_list[0], (NSEQ, SEQ_LEN, D), 1.0, 6.0, ((0, 8), (1, 4)))
    out_cotangent = normal_values(key_list[1], (NSEQ, SEQ_LEN, D), 1.0, 6.0, ((0, 8), (1, 4)))
    expert_ids_keys = jax.random.split(jax.random.fold_in(key_list[2], 1), LAYERS * (N_DP * N_EXP) * N_CTX * (SEQS * BLK) // (SEQS * BLK))
    expert_ids_turns = jax.random.permutation(jax.random.fold_in(key_list[2], 3), LAYERS * (N_DP * N_EXP) * N_CTX * (SEQS * BLK) // (SEQS * BLK))
    expert_ids = jax.vmap(lambda own, number: routed_block(jax.random.fold_in(key_list[2], 2), own, number, SEQS * BLK, EXPERTS, 1, CAP, 2))(expert_ids_keys, expert_ids_turns).reshape((LAYERS, N_DP * N_EXP, N_CTX, SEQS * BLK, 1))
    rel_buckets = set_ends(jax.random.randint(key_list[3], (2 * SEQ_LEN - 1,), 0, NB), jax.random.fold_in(key_list[3], 1), 0, NB - 1).astype(jnp.int32)
    bias_table = normal_values(key_list[4], (NB, H), 1.0, 6.0)
    gain_attn = jnp.clip(1.0 + 0.1 * jax.random.normal(key_list[5], (LAYERS, D), jnp.float32), 0.5, 1.5).astype(jnp.bfloat16)
    w_query = normal_values(key_list[6], (LAYERS, D, HD), D ** -0.5, 0.21875, ((1, 4),))
    w_key = normal_values(key_list[7], (LAYERS, D, HD), D ** -0.5, 0.21875, ((1, 4),))
    w_value = normal_values(key_list[8], (LAYERS, D, HD), D ** -0.5, 0.21875, ((1, 4),))
    w_output = normal_values(key_list[9], (LAYERS, HD, D), (max(HD // 256, 1)) ** -0.5, 3.5, ((1, 4),))
    gain_ffn = jnp.clip(1.0 + 0.1 * jax.random.normal(key_list[10], (LAYERS, D), jnp.float32), 0.5, 1.5).astype(jnp.bfloat16)
    w_router = normal_values(key_list[11], (LAYERS, D, EXPERTS), (4 * D) ** -0.5, 0.109375, ((1, 4),))
    w_inner = normal_values(key_list[12], (LAYERS, EXPERTS, D, FF), D ** -0.5, 0.21875, ((1, 2), (2, 4)))
    w_outer = normal_values(key_list[13], (LAYERS, EXPERTS, FF, D), (max(FF // 48, 1)) ** -0.5, 0.75, ((1, 2), (2, 4)))
    return dict(block_input=block_input, out_cotangent=out_cotangent, expert_ids=expert_ids, rel_buckets=rel_buckets, bias_table=bias_table, gain_attn=gain_attn, w_query=w_query, w_key=w_key, w_value=w_value, w_output=w_output, gain_ffn=gain_ffn, w_router=w_router, w_inner=w_inner, w_outer=w_outer)


NORM_EPSILON = 1e-06
PRECISION_HIGH = lax.Precision.HIGHEST

@jax.custom_vjp
def low(v):
    return lax.optimization_barrier(v.astype(jnp.bfloat16)).astype(jnp.float32)

@jax.custom_vjp
def low_back(v):
    return v

def low_keep(v):
    return (low(v), None)

def low_pass(kept, grad):
    return (grad,)

def back_keep(v):
    return (v, None)

def back_low(kept, grad):
    return (low(grad),)
low.defvjp(low_keep, low_pass)
low_back.defvjp(back_keep, back_low)

def rms_norm(values, gain):
    return values * lax.rsqrt(lax.optimization_barrier(jnp.mean(values * values, axis=-1, keepdims=True)) + NORM_EPSILON) * gain

def product(left, right):
    return jnp.matmul(left, right, precision=PRECISION_HIGH)

def to_blocks(values):
    groups = N_DP * N_EXP
    shaped = values.reshape(groups, SEQS, N_CTX, BLK, values.shape[-1])
    return jnp.transpose(shaped, (0, 2, 1, 3, 4)).reshape(groups, N_CTX, SEQS * BLK, values.shape[-1])

def from_blocks(values):
    groups = N_DP * N_EXP
    shaped = values.reshape(groups, N_CTX, SEQS, BLK, values.shape[-1])
    return jnp.transpose(shaped, (0, 2, 1, 3, 4)).reshape(groups * SEQS, N_CTX * BLK, values.shape[-1])

def slot_targets(expert_row):
    onehot = (expert_row[:, None] == jnp.arange(EXPERTS, dtype=jnp.int32)[None, :]).astype(jnp.int32)
    rank_before = jnp.cumsum(onehot, axis=0) - onehot
    return (expert_row * CAP + lax.optimization_barrier(jnp.sum(rank_before * onehot, axis=1))).astype(jnp.int32)

def place_rows(values, targets):
    return jnp.zeros((EXPERTS * CAP, values.shape[-1]), jnp.float32).at[targets].set(values)

def pick_rows(values, targets):
    return values[targets]

def attend_one(block_items, bias_heads):
    query_low, key_low, value_low = block_items
    query_heads = query_low.reshape(SEQ_LEN, H, DH)
    key_heads = key_low.reshape(SEQ_LEN, H, DH)
    value_heads = value_low.reshape(SEQ_LEN, H, DH)
    raw_scores = low_back(jnp.einsum('qhd,khd->hqk', query_heads, key_heads, precision=PRECISION_HIGH))
    scores = raw_scores * DH ** (-0.5) + bias_heads
    probabilities = jax.nn.softmax(scores, axis=-1)
    mixed_heads = jnp.einsum('hqk,khd->qhd', low(probabilities), value_heads, precision=PRECISION_HIGH)
    return low(low_back(mixed_heads.reshape(SEQ_LEN, HD)))

def layer_forward(stream, bias_heads, layer_weights, targets, expert_hot):
    gain_one, query_weight, key_weight, value_weight, output_weight, gain_two, router_weight, inner_weight, outer_weight = layer_weights
    normed_one = low(rms_norm(stream, gain_one))
    query_low = low(low_back(product(normed_one, query_weight)))
    key_low = low(low_back(product(normed_one, key_weight)))
    value_low = low(low_back(product(normed_one, value_weight)))
    attend = jax.checkpoint(partial(attend_one, bias_heads=bias_heads))
    mixed_low = lax.map(attend, (query_low, key_low, value_low))
    mid_stream = stream + low_back(product(mixed_low, output_weight))
    normed_two = low(rms_norm(mid_stream, gain_two))
    logits = low_back(product(normed_two, router_weight))
    router_probs = jax.nn.softmax(logits, axis=-1)
    block_rows = to_blocks(normed_two)
    gate_value = lax.optimization_barrier(jnp.sum(to_blocks(router_probs) * expert_hot, axis=-1, keepdims=True))
    groups = N_DP * N_EXP
    buffers = jax.vmap(jax.vmap(place_rows))(block_rows, targets).reshape(groups, N_CTX, EXPERTS, CAP, D)
    pre_act = low_back(jnp.einsum('gcerd,edf->gcerf', buffers, inner_weight, precision=PRECISION_HIGH))
    activated = low(jax.nn.gelu(pre_act, approximate=True))
    expert_out = low(low_back(jnp.einsum('gcerf,efd->gcerd', activated, outer_weight, precision=PRECISION_HIGH)))
    returned = jax.vmap(jax.vmap(pick_rows))(expert_out.reshape(groups, N_CTX, EXPERTS * CAP, D), targets)
    return mid_stream + from_blocks(gate_value * returned)

def forward(block_input, bias_table, gain_attn, w_query, w_key, w_value, w_output, gain_ffn, w_router, w_inner, w_outer, rel_buckets, expert_ids):
    position = jnp.arange(SEQ_LEN, dtype=jnp.int32)
    offsets = position[None, :] - position[:, None] + SEQ_LEN - 1
    bias_heads = jnp.transpose(bias_table[rel_buckets[offsets]], (2, 0, 1))
    stream = block_input
    for layer_id in range(LAYERS):
        routes_now = expert_ids[layer_id, :, :, :, 0]
        targets = jax.vmap(jax.vmap(slot_targets))(routes_now)
        expert_hot = (routes_now[..., None] == jnp.arange(EXPERTS, dtype=jnp.int32)).astype(jnp.float32)
        layer_weights = (gain_attn[layer_id], w_query[layer_id], w_key[layer_id], w_value[layer_id], w_output[layer_id], gain_ffn[layer_id], w_router[layer_id], w_inner[layer_id], w_outer[layer_id])
        stream = layer_forward(stream, bias_heads, layer_weights, targets, expert_hot)
    return stream

def reference(block_input, out_cotangent, expert_ids, rel_buckets, bias_table, gain_attn, w_query, w_key, w_value, w_output, gain_ffn, w_router, w_inner, w_outer):
    bound = partial(forward, rel_buckets=rel_buckets, expert_ids=expert_ids)
    output, pullback = jax.vjp(bound, block_input.astype(jnp.float32), bias_table.astype(jnp.float32), gain_attn.astype(jnp.float32), w_query.astype(jnp.float32), w_key.astype(jnp.float32), w_value.astype(jnp.float32), w_output.astype(jnp.float32), gain_ffn.astype(jnp.float32), w_router.astype(jnp.float32), w_inner.astype(jnp.float32), w_outer.astype(jnp.float32))
    gradients = pullback(out_cotangent.astype(jnp.float32))
    return (output.astype(jnp.bfloat16), gradients[0], gradients[2], gradients[3], gradients[4], gradients[5], gradients[6], gradients[7], gradients[8], gradients[9], gradients[10], gradients[1])
```

```python
from functools import partial

import jax
import jax.numpy as jnp
from jax import lax
from jax.experimental import pallas as pl
from jax.experimental.pallas import tpu as pltpu
from jax.sharding import PartitionSpec as P

NORM_EPSILON = 1e-06
PRECISION_HIGH = lax.Precision.HIGHEST
LANES = 128
FOLD_ROWS = 8
VMEM_BYTES = 56 * 2**20
F32 = jnp.float32
BF16 = jnp.bfloat16


def rms_norm(values, gain):
    return (
        values * lax.rsqrt(jnp.mean(values * values, axis=-1, keepdims=True) + NORM_EPSILON) * gain
    )


def dot_f32(left, right, dims):
    return lax.dot_general(left, right, (dims, ((), ())), preferred_element_type=F32)


def head_mask(head, head_dim):
    lane = lax.broadcasted_iota(jnp.int32, (1, LANES), 1)
    return (lane >= head * head_dim) & (lane < (head + 1) * head_dim)


def masked(values, mask):
    return jnp.where(mask, values.astype(F32), 0.0).astype(BF16)


def head_scores(query, key, seg_row, scale):
    rows, width = query.shape[0], seg_row.shape[1]
    wide = jnp.broadcast_to(seg_row, (rows, width))
    bias = pltpu.roll(wide, width - (rows - 1), 1, stride=1, stride_axis=0)
    return dot_f32(query, key, ((1,), (1,))) * scale + bias[:, : key.shape[0]]


def forward_kernel(head_dim, seg_ref, query_ref, key_ref, value_ref, out_ref):
    scale = head_dim ** (-0.5)
    query, key, value = query_ref[...], key_ref[...], value_ref[...]
    out = jnp.zeros(out_ref.shape, F32)
    for head in range(LANES // head_dim):
        mask = head_mask(head, head_dim)
        scores = head_scores(masked(query, mask), key, seg_ref[head], scale)
        weights = jnp.exp(scores - jnp.max(scores, axis=-1, keepdims=True))
        total = jnp.sum(weights, axis=-1, keepdims=True)
        mixed = dot_f32(weights.astype(BF16), value, ((1,), (0,))) / total
        out = jnp.where(mask, mixed, out)
    out_ref[...] = out.astype(BF16)


def backward_kernel(
    head_dim, seg_ref, query_ref, key_ref, value_ref, grad_ref, dq_ref, dkv_ref, dseg_ref
):
    scale = head_dim ** (-0.5)
    query, key, value, grad = query_ref[...], key_ref[...], value_ref[...], grad_ref[...]
    rows = query.shape[0]
    dq = jnp.zeros(dq_ref.shape, F32)
    dk = jnp.zeros(key.shape, F32)
    dv = jnp.zeros(key.shape, F32)
    for head in range(LANES // head_dim):
        mask = head_mask(head, head_dim)
        query_h, grad_h = masked(query, mask), masked(grad, mask)
        scores = head_scores(query_h, key, seg_ref[head], scale)
        weights = jnp.exp(scores - jnp.max(scores, axis=-1, keepdims=True))
        probs = weights * (1.0 / jnp.sum(weights, axis=-1, keepdims=True))
        prob_grad = dot_f32(grad_h, value, ((1,), (1,)))
        delta = jnp.sum(probs * prob_grad, axis=-1, keepdims=True)
        score_grad = probs * (prob_grad - delta)
        raw_grad = (score_grad * scale).astype(BF16)
        dq = jnp.where(mask, dot_f32(raw_grad, key, ((1,), (0,))), dq)
        dk = dk + dot_f32(raw_grad, query_h, ((0,), (0,)))
        dv = dv + dot_f32(probs.astype(BF16), grad_h, ((0,), (0,)))
        fold = jnp.concatenate([score_grad, jnp.zeros((rows, rows), F32)], axis=1)
        half = rows // 2
        while half >= FOLD_ROWS:
            fold = pltpu.roll(fold[:half], half, 1) + fold[half:]
            half //= 2
        dseg_ref[head] = fold
    dq_ref[...] = dq.astype(BF16)
    dkv_ref[0] = dk.astype(BF16)
    dkv_ref[1] = dv.astype(BF16)


def attention_specs(rows, span, width, hidden, per_block):
    blocks = hidden // LANES
    return [
        pl.BlockSpec((per_block, 1, width), lambda b: (b, 0, 0)),
        pl.BlockSpec((rows, LANES), lambda b: (0, b)),
        pl.BlockSpec((span, LANES), lambda b: (0, b)),
        pl.BlockSpec((span, LANES), lambda b: (0, b + blocks)),
    ]


def attention_forward(segments, query, keys_values):
    heads, _, width = segments.shape
    rows, hidden = query.shape
    span = keys_values.shape[0]
    head_dim = hidden // heads
    per_block = LANES // head_dim
    return pl.pallas_call(
        partial(forward_kernel, head_dim),
        grid=(hidden // LANES,),
        in_specs=attention_specs(rows, span, width, hidden, per_block),
        out_specs=pl.BlockSpec((rows, LANES), lambda b: (0, b)),
        out_shape=jax.ShapeDtypeStruct((rows, hidden), BF16),
        compiler_params=pltpu.CompilerParams(vmem_limit_bytes=VMEM_BYTES),
        cost_estimate=pl.CostEstimate(
            flops=8 * rows * span * hidden, bytes_accessed=4 * span * hidden, transcendentals=0
        ),
    )(segments, query, keys_values, keys_values)


def attention_backward(segments, query, keys_values, mix_grad):
    heads, _, width = segments.shape
    rows, hidden = query.shape
    span = keys_values.shape[0]
    head_dim = hidden // heads
    per_block = LANES // head_dim
    return pl.pallas_call(
        partial(backward_kernel, head_dim),
        grid=(hidden // LANES,),
        in_specs=attention_specs(rows, span, width, hidden, per_block)
        + [pl.BlockSpec((rows, LANES), lambda b: (0, b))],
        out_specs=[
            pl.BlockSpec((rows, LANES), lambda b: (0, b)),
            pl.BlockSpec((2, span, LANES), lambda b: (0, 0, b)),
            pl.BlockSpec((per_block, FOLD_ROWS, width), lambda b: (b, 0, 0)),
        ],
        out_shape=[
            jax.ShapeDtypeStruct((rows, hidden), BF16),
            jax.ShapeDtypeStruct((2, span, hidden), BF16),
            jax.ShapeDtypeStruct((heads, FOLD_ROWS, width), F32),
        ],
        compiler_params=pltpu.CompilerParams(vmem_limit_bytes=VMEM_BYTES),
        cost_estimate=pl.CostEstimate(
            flops=20 * rows * span * hidden, bytes_accessed=8 * span * hidden, transcendentals=0
        ),
    )(segments, query, keys_values, keys_values, mix_grad)


def dispatch_onehot(ids, first_expert, local_experts, capacity):
    slots = []
    for local in range(local_experts):
        match = (ids == first_expert + local).astype(jnp.int32)
        rank = jnp.cumsum(match, axis=1) - match
        slots.append(jnp.where(match == 1, rank, -1))
    slot = jnp.stack(slots)
    return (
        slot[:, :, None, :] == jnp.arange(capacity, dtype=jnp.int32)[None, None, :, None]
    ).astype(BF16)


def to_experts(onehot, tokens):
    experts, groups, capacity, rows = onehot.shape
    grouped = tokens.reshape(groups, rows, tokens.shape[-1])
    picked = jnp.einsum("egst,gtd->egsd", onehot, grouped, preferred_element_type=F32)
    return picked.astype(BF16).reshape(experts, groups * capacity, tokens.shape[-1])


def to_tokens(onehot, slots):
    experts, groups, capacity, rows = onehot.shape
    grouped = slots.reshape(experts, groups, capacity, slots.shape[-1])
    placed = jnp.einsum("egst,egsd->gtd", onehot, grouped, preferred_element_type=F32)
    return placed.astype(BF16).reshape(groups * rows, slots.shape[-1])


def gather_tokens(rows):
    return lax.all_gather(rows, ("dp", "exp"), axis=0, tiled=True)


def sum_tokens(rows):
    return lax.psum_scatter(rows, ("dp", "exp"), scatter_dimension=0, tiled=True)


def sum_scattered(partial_sum, axes):
    flat = partial_sum.reshape(-1, partial_sum.shape[-1])
    return lax.psum_scatter(flat, axes, scatter_dimension=0, tiled=True)


def shared_sums(own_sums):
    attn_own, inner_own, outer_own = own_sums
    return (
        lax.all_gather(attn_own, ("ctx", "exp"), axis=0, tiled=True),
        lax.all_gather(inner_own, "ctx", axis=0, tiled=True),
        lax.all_gather(outer_own, "ctx", axis=0, tiled=True),
    )


def layer_forward(stream, weights, segments, route_row, onehot, experts_all):
    gain_one, gain_two, router_weight, attn_weight, inner_weight, outer_weight = weights
    width = stream.shape[1]
    normed_one = rms_norm(stream, gain_one).astype(BF16)
    key_value = dot_f32(normed_one, attn_weight[:, width : 3 * width], ((1,), (0,))).astype(BF16)
    keys_values = lax.all_gather(key_value, "ctx", axis=0, tiled=True)
    query = dot_f32(normed_one, attn_weight[:, :width], ((1,), (0,))).astype(BF16)
    mixed = attention_forward(segments, query, keys_values)
    mid = stream + dot_f32(mixed, attn_weight[:, 3 * width :], ((1,), (0,)))
    normed_two = rms_norm(mid, gain_two).astype(BF16)
    tokens = gather_tokens(normed_two)
    router_probs = jax.nn.softmax(dot_f32(normed_two, router_weight, ((1,), (0,))), axis=-1)
    expert_hot = (route_row[:, None] == jnp.arange(experts_all, dtype=jnp.int32)[None, :]).astype(
        F32
    )
    gate = jnp.sum(router_probs * expert_hot, axis=-1, keepdims=True)
    received = to_experts(onehot, tokens)
    pre_act = jnp.einsum("erd,edf->erf", received, inner_weight, preferred_element_type=F32)
    activated = jax.nn.gelu(pre_act, approximate=True).astype(BF16)
    expert_out = jnp.einsum(
        "erf,efd->erd", activated, outer_weight, preferred_element_type=F32
    ).astype(BF16)
    returned = sum_tokens(to_tokens(onehot, expert_out))
    new_stream = mid + gate * returned.astype(F32)
    saved = (
        stream,
        normed_one,
        query,
        keys_values,
        mixed,
        mid,
        normed_two,
        router_probs,
        expert_hot,
        gate,
        received,
        pre_act,
        activated,
        returned,
    )
    return (new_stream, saved)


def layer_backward(grad_stream, saved, weights, segments, onehot, pending):
    gain_one, gain_two, router_weight, attn_weight, inner_weight, outer_weight = weights
    (
        stream,
        normed_one,
        query,
        keys_values,
        mixed,
        mid,
        normed_two,
        router_probs,
        expert_hot,
        gate,
        received,
        pre_act,
        activated,
        returned,
    ) = saved
    width = stream.shape[1]
    out_grad = (gate * grad_stream).astype(BF16)
    expert_grad = to_experts(onehot, gather_tokens(out_grad))
    gate_grad = jnp.sum(grad_stream * returned.astype(F32), axis=-1, keepdims=True)
    act_grad = jnp.einsum("erd,efd->erf", expert_grad, outer_weight, preferred_element_type=F32)
    pre_grad = jax.vjp(partial(jax.nn.gelu, approximate=True), pre_act)[1](act_grad)[0].astype(BF16)
    token_part = jnp.einsum(
        "erf,edf->erd", pre_grad, inner_weight, preferred_element_type=F32
    ).astype(BF16)
    token_back = sum_tokens(to_tokens(onehot, token_part)).astype(F32)
    outer_grad = jnp.einsum(
        "erf,erd->efd", activated, expert_grad, preferred_element_type=F32
    ).astype(BF16)
    inner_grad = jnp.einsum("erd,erf->edf", received, pre_grad, preferred_element_type=F32).astype(
        BF16
    )
    inner_grad = lax.all_to_all(inner_grad, "dp", split_axis=1, concat_axis=2, tiled=True)
    outer_grad = sum_scattered(outer_grad, "ctx")
    inner_grad = sum_scattered(inner_grad, "ctx")
    logit_grad = (router_probs * (expert_hot - gate) * gate_grad).astype(BF16)
    router_grad = dot_f32(normed_two, logit_grad, ((0,), (0,)))
    two_grad = dot_f32(logit_grad, router_weight, ((1,), (1,))) + token_back
    mid_part, gain_two_grad = jax.vjp(rms_norm, mid, gain_two)[1](two_grad)
    mid_grad = grad_stream + mid_part
    attn_grad = mid_grad.astype(BF16)
    mix_grad = dot_f32(attn_grad, attn_weight[:, 3 * width :], ((1,), (1,))).astype(BF16)
    if pending is not None:
        mix_grad, pending = lax.optimization_barrier((mix_grad, pending))
        pending = shared_sums(pending)
    query_grad, key_value_grad, dseg = attention_backward(segments, query, keys_values, mix_grad)
    key_value_grad = lax.psum_scatter(key_value_grad, "ctx", scatter_dimension=1, tiled=True)
    if pending is not None:
        key_value_grad, pending = lax.optimization_barrier((key_value_grad, pending))
    output_grad = dot_f32(mixed, attn_grad, ((0,), (0,))).astype(BF16)
    joined = jnp.concatenate([query_grad, key_value_grad[0], key_value_grad[1]], axis=1)
    qkv_grad = dot_f32(normed_one, joined, ((0,), (0,))).astype(BF16)
    one_grad = dot_f32(joined, attn_weight[:, : 3 * width], ((1,), (1,)))
    attn_weight_grad = lax.psum_scatter(
        jnp.concatenate([qkv_grad, output_grad], axis=1), "dp", scatter_dimension=0, tiled=True
    )
    attn_weight_grad = sum_scattered(attn_weight_grad, ("ctx", "exp"))
    stream_part, gain_one_grad = jax.vjp(rms_norm, stream, gain_one)[1](one_grad)
    small = jnp.concatenate([gain_one_grad[:, None], gain_two_grad[:, None], router_grad], axis=1)
    sums = (attn_weight_grad, inner_grad, outer_grad)
    return (mid_grad + stream_part, sums, pending, small, dseg)


def shards(
    block_input,
    out_cotangent,
    expert_ids,
    rel_buckets,
    bias_table,
    gain_attn,
    w_query,
    w_key,
    w_value,
    w_output,
    gain_ffn,
    w_router,
    w_inner,
    w_outer,
):
    layer_count = gain_attn.shape[0]
    bucket_count, head_count = bias_table.shape
    local_experts = w_inner.shape[1]
    experts_all = local_experts * lax.axis_size("exp")
    rows, width = block_input.shape[0] * block_input.shape[1], block_input.shape[2]
    capacity = 2 * rows // experts_all
    span = rows * lax.axis_size("ctx")
    ctx_index, dp_index = lax.axis_index("ctx"), lax.axis_index("dp")
    shard_rows = w_query.shape[1]

    attn_full = [
        lax.all_gather(
            jnp.concatenate([w_query[l], w_key[l], w_value[l], w_output[l]], axis=1),
            "dp",
            axis=0,
            tiled=True,
        )
        for l in range(layer_count)
    ]
    vectors = lax.all_gather(
        jnp.concatenate([gain_attn[..., None], gain_ffn[..., None], w_router], axis=2),
        "dp",
        axis=1,
        tiled=True,
    )
    ids_all = lax.all_gather(
        expert_ids.reshape(layer_count, 1, rows), ("dp", "exp"), axis=1, tiled=True
    )
    inner_full = [
        lax.all_to_all(w_inner[l], "dp", split_axis=2, concat_axis=1, tiled=True)
        for l in range(layer_count)
    ]

    seg_len = span + rows - 1
    seg_ids = lax.dynamic_slice_in_dim(rel_buckets, span - rows - ctx_index * rows, seg_len)
    seg_ids = jnp.concatenate([seg_ids, jnp.full((1,), -1, jnp.int32)])
    seg_hot = (seg_ids[None, :] == jnp.arange(bucket_count, dtype=jnp.int32)[:, None]).astype(F32)
    segments = jnp.einsum(
        "bh,bm->hm", bias_table.astype(F32), seg_hot, precision=PRECISION_HIGH
    )[:, None, :]

    first_expert = lax.axis_index("exp") * local_experts
    onehots = [
        dispatch_onehot(ids_all[l], first_expert, local_experts, capacity)
        for l in range(layer_count)
    ]
    weights = [
        (
            vectors[l, :, 0].astype(F32),
            vectors[l, :, 1].astype(F32),
            vectors[l, :, 2:],
            attn_full[l],
            inner_full[l],
            w_outer[l],
        )
        for l in range(layer_count)
    ]
    stream = block_input.reshape(rows, width).astype(F32)
    kept = []
    for l in range(layer_count):
        stream, saved = layer_forward(
            stream, weights[l], segments, expert_ids[l].reshape(rows), onehots[l], experts_all
        )
        kept.append(saved)
    block_output = stream.astype(BF16).reshape(block_input.shape)

    grad_stream = out_cotangent.reshape(rows, width).astype(F32)
    shared = [None] * layer_count
    smalls = [None] * layer_count
    dseg8 = jnp.zeros((), F32)
    pending = None
    for l in reversed(range(layer_count)):
        grad_stream, sums, done, smalls[l], dseg_part = layer_backward(
            grad_stream, kept[l], weights[l], segments, onehots[l], pending
        )
        if done is not None:
            shared[l + 1] = done
        pending = sums
        dseg8 = dseg8 + dseg_part
    shared[0] = shared_sums(pending)
    attn_grads = jnp.stack([part[0] for part in shared]).astype(F32)
    inner_grads = jnp.stack([part[1].reshape(w_inner.shape[1:]) for part in shared]).astype(F32)
    outer_grads = jnp.stack([part[2].reshape(w_outer.shape[1:]) for part in shared]).astype(F32)
    small = jnp.stack(smalls)
    dseg = sum(jnp.roll(dseg8[:, i, :], FOLD_ROWS - 1 - i, axis=-1) for i in range(FOLD_ROWS))
    table_grad = jnp.einsum("bm,hm->bh", seg_hot, dseg, precision=PRECISION_HIGH)
    flat = lax.psum(
        jnp.concatenate([small.reshape(-1), table_grad.reshape(-1)]), ("dp", "ctx", "exp")
    )
    small = lax.dynamic_slice_in_dim(
        flat[: small.size].reshape(small.shape), dp_index * shard_rows, shard_rows, axis=1
    )
    heads_local = head_count // lax.axis_size("dp")
    table_grad = lax.dynamic_slice_in_dim(
        flat[-table_grad.size :].reshape(table_grad.shape),
        dp_index * heads_local,
        heads_local,
        axis=1,
    )
    return (
        block_output,
        grad_stream.reshape(block_input.shape),
        small[:, :, 0],
        attn_grads[:, :, :width],
        attn_grads[:, :, width : 2 * width],
        attn_grads[:, :, 2 * width : 3 * width],
        attn_grads[:, :, 3 * width :],
        small[:, :, 1],
        small[:, :, 2:],
        inner_grads,
        outer_grads,
        table_grad,
    )


def solution(mesh):
    in_specs = (
        P(("dp", "exp"), "ctx", None),
        P(("dp", "exp"), "ctx", None),
        P(None, ("dp", "exp"), "ctx", None, None),
        P(),
        P(),
        P(None, "dp"),
        P(None, "dp", None),
        P(None, "dp", None),
        P(None, "dp", None),
        P(None, "dp", None),
        P(None, "dp"),
        P(None, "dp", None),
        P(None, "exp", "dp", None),
        P(None, "exp", "dp", None),
    )
    out_specs = (
        P(("dp", "exp"), "ctx", None),
        P(("dp", "exp"), "ctx", None),
        P(None, "dp"),
        P(None, "dp", None),
        P(None, "dp", None),
        P(None, "dp", None),
        P(None, "dp", None),
        P(None, "dp"),
        P(None, "dp", None),
        P(None, "exp", "dp", None),
        P(None, "exp", "dp", None),
        P(None, "dp"),
    )
    return jax.shard_map(shards, mesh=mesh, in_specs=in_specs, out_specs=out_specs, check_vma=False)
```
